256 devices in a mesh: date: 16 (over z, core), tile: 16 (over x, y).
Axes of the slice: x: 4, y: 4, z: 8, core: 2. Of those that a mesh axis runs over, the one named last changes fastest.
Arguments:
- slc: float32 [208, 2, 128, 8192], P('date', None, None, 'tile'), as said below
- pair_slots: int32 [1024, 2], P('date'), may hold values from -1 to 207, as said below
- inversion: float32 [207, 1024], P(None, 'date'), may hold values from -0.5 to 0.5
Outputs:
- series: float32 [16, 207, 4096], P('date', None, 'tile')
The draws below stay inside these ranges and needn't reach their ends.
Inputs may be any that keep to these rules, and one draw needn't show every extreme that they name: `pair_slots`: slot s belongs to owner s // 64. A live slot holds a reference acquisition r inside its owner's block of 13 acquisitions and a secondary r + k with 1 <= k <= 4; no pair appears twice. An owner has at most 52 live slots, and some owner has exactly that many. Live slots come first among an owner's slots; empty slots hold -1 in both columns. `slc`: real parts are positive and every phase atan2(imaginary, real) lies within 0.45 of zero.
All inputs are finite; a program needn't handle non-finite values.
Results may differ from the reference program's by a relative error of at most 0.000073.
Values sent between devices are 32-bit elements; how exact they have to be, the bound alone decides.
No kernel may reach another device: no remote copies, remote signals or barrier semaphores. Data moves between devices by JAX's collectives and lax.ppermute only.
A program may use at most 128 MiB of HBM per device.

```python
import jax
import jax.numpy as jnp
from jax import lax

DATES_DEV = 13
SPAN = 4
LINES = 128
PAIR_CAP = 64
DATES = 208
COLS = 8192
SLOTS = 1024
N_DATE = 16


def draw_pair_slots(key, part):
    key = jax.random.fold_in(key, 11)
    keys = jax.random.split(key, 3)
    cand = DATES_DEV * SPAN
    owners = jnp.arange(N_DATE, dtype=jnp.int32)
    index = jnp.arange(cand, dtype=jnp.int32)
    ref_date = owners[:, None] * DATES_DEV + (index // SPAN)[None, :]
    sec_date = ref_date + (index % SPAN + 1)[None, :]
    valid = sec_date <= DATES - 1
    rate = jax.random.randint(keys[0], (N_DATE, 1), 0, 21)
    roll = jax.random.randint(keys[1], (N_DATE, cand), 0, 100)
    full = jax.random.randint(keys[2], (), 0, N_DATE - 1)
    keep = valid & ((roll >= rate) | (owners[:, None] == full))
    order = jnp.argsort(jnp.where(keep, index[None, :], index[None, :] + cand), axis=1)
    ref_date = jnp.take_along_axis(ref_date, order, 1)
    sec_date = jnp.take_along_axis(sec_date, order, 1)
    keep = jnp.take_along_axis(keep, order, 1)
    ref_date = jnp.where(keep, ref_date, -1)
    sec_date = jnp.where(keep, sec_date, -1)
    padding = -jnp.ones((N_DATE, PAIR_CAP - cand), jnp.int32)
    ref_date = jnp.concatenate([ref_date, padding], 1)
    sec_date = jnp.concatenate([sec_date, padding], 1)
    return jnp.stack([ref_date, sec_date], -1).reshape(N_DATE * PAIR_CAP, 2).astype(jnp.int32)


def draw_slc(key, part):
    key = jax.random.fold_in(key, 23)
    keys = jax.random.split(key, 3)
    shape = (DATES, LINES, COLS)
    column = jnp.arange(COLS, dtype=jnp.float32) / COLS
    ramp = jax.random.uniform(keys[1], (DATES,), jnp.float32, -0.18, 0.18)
    rough = jax.random.uniform(keys[2], shape, jnp.float32, -0.15, 0.15)
    phase = ramp[:, None, None] * column[None, None, :] + rough
    amplitude = jnp.exp(jax.random.uniform(keys[0], shape, jnp.float32, -1.0, 1.0))
    return jnp.stack([amplitude * jnp.cos(phase), amplitude * jnp.sin(phase)], 1).astype(jnp.float32)


def block_scale(stream_key, shape, shards, low, largest):
    def one(position, parts):
        draws = jax.random.uniform(jax.random.fold_in(jax.random.fold_in(stream_key, 6), position), (parts,), jnp.float32, low / len(shards), largest / len(shards))
        return jnp.repeat(jnp.exp(draws), shape[position] // parts).reshape((-1,) + (1,) * (len(shape) - position - 1))

    gain = one(*shards[0])
    for cut in shards[1:]:
        gain = gain * one(*cut)
    return gain


def gaussian(key, shape, spread, limit, cuts=(), held_as=jnp.bfloat16):
    result = jax.random.normal(key, shape, jnp.float32) * spread
    if len(cuts) > 0:
        result = block_scale(key, shape, cuts, -0.22, 0.18) * result
    return jnp.clip(result, min=-limit, max=limit).astype(held_as)


def setup_inputs(seed: int = 0) -> dict:
    key_list = jax.random.split(jax.random.key(seed), 4)
    slc = draw_slc(jax.random.fold_in(key_list[3], 71), 0)
    pair_slots = draw_pair_slots(jax.random.fold_in(key_list[3], 71), 0)
    inversion = gaussian(key_list[2], (DATES - 1, SLOTS), (N_DATE * PAIR_CAP // 8) ** -0.5, 0.5, ((1, 16),), jnp.float32)
    return {"slc": slc, "pair_slots": pair_slots, "inversion": inversion}


def reference(slc, pair_slots, inversion):
    live = pair_slots[:, 0] >= 0
    ref_date = jnp.maximum(pair_slots[:, 0], 0).astype(jnp.int32)
    sec_date = jnp.maximum(pair_slots[:, 1], 0).astype(jnp.int32)
    lines = slc.shape[2]
    cols = slc.shape[3]

    def one_pair(index_pair):
        first = slc[index_pair[0]]
        second = slc[index_pair[1]]
        real_part = first[0] * second[0] + first[1] * second[1]
        imag_part = first[1] * second[0] - first[0] * second[1]
        stacked = jnp.stack([real_part, imag_part])
        return stacked.reshape(2, lines // 8, 8, cols // 2, 2).sum(axis=(2, 4))

    looked = lax.map(one_pair, jnp.stack([ref_date, sec_date], 1))
    phase = jnp.where(live[:, None, None], jnp.arctan2(looked[:, 1], looked[:, 0]), jnp.zeros((), looked.dtype))
    offset = jnp.mean(phase, axis=(1, 2))
    centred = phase - offset[:, None, None]
    return jnp.einsum("ts,slc->ltc", inversion, centred, precision=lax.Precision.HIGHEST)
```

```python
import jax
import jax.numpy as jnp
from jax import lax
from jax.experimental import pallas as pl
from jax.experimental.pallas import tpu as pltpu
from jax.sharding import PartitionSpec as P

N = 16
DATES_DEV = 13
SPAN = 4
LINES = 16
LANES = 128
CUT = 0.41421356

LATE = [(10, 12), (11, 12)]
AHEAD = [(9, 13), (10, 13), (10, 14), (11, 13), (11, 14), (12, 13), (12, 14)]
BACK = [(11, 15), (12, 15), (12, 16)]
EARLY = [
    (r, r + k)
    for r in range(DATES_DEV)
    for k in range(1, SPAN + 1)
    if r + k < DATES_DEV and (r, r + k) not in LATE
]
ORDER = EARLY + LATE + AHEAD + BACK
N_EARLY = len(EARLY)
N_ALL = len(ORDER)
PAD = 56
ROWS = 2 * PAD
DEPTH = N * PAD
TIMES = 208


def angle(re, im):
    size = jnp.abs(im)
    big = size > CUT * re
    num = jnp.where(big, size - re, size)
    den = jnp.where(big, size + re, re)
    t = num / den
    z = t * t
    p = ((8.05374449538e-2 * z - 1.38776856032e-1) * z + 1.99777106478e-1) * z - 3.33329491539e-1
    y = p * z * t + t
    y = jnp.where(big, y + 0.7853981633974483, y)
    y = jnp.where(im < 0, -y, y)
    return jnp.where(re > 0, y, 0.0)


def lane_iota():
    return lax.broadcasted_iota(jnp.int32, (8, LANES), 1)


def form(load, pairs):
    lane = lane_iota()
    even = (lane & 1) == 0
    swap = lane ^ 1
    by_ref = {}
    for n, (r, q) in enumerate(pairs):
        by_ref.setdefault(r, []).append((n, q))
    for r, members in by_ref.items():
        acc = {}
        for side in range(2):
            for j in range(8):
                a, b = load(side, r, 0, j), load(side, r, 1, j)
                for n, q in members:
                    c, d = load(side, q, 0, j), load(side, q, 1, j)
                    re = a * c + b * d
                    im = b * c - a * d
                    if j:
                        re = acc[n, side, 0] + re
                        im = acc[n, side, 1] + im
                    acc[n, side, 0], acc[n, side, 1] = re, im
        for n, _ in members:
            looked = []
            for part in range(2):
                left, right = acc[n, 0, part], acc[n, 1, part]
                kept = jnp.where(even, left, right)
                other = jnp.where(even, right, left)
                looked.append(kept + jnp.take_along_axis(other, swap, axis=1))
            yield n, angle(looked[0], looked[1])


def early_kernel(left_ref, right_ref, out_ref, sum_ref):
    g, h = pl.program_id(0), pl.program_id(1)
    first = jnp.logical_and(g == 0, h == 0)

    @pl.when(first)
    def _():
        sum_ref[...] = jnp.zeros_like(sum_ref)

    refs = (left_ref, right_ref)

    def load(side, date, part, j):
        return refs[side][date, part, pl.ds(j, 8, stride=8), :]

    for n, phase in form(load, EARLY):
        start = g * (8 * 2 * N_EARLY) + h * N_EARLY + n
        out_ref[pl.ds(start, 8, stride=2 * N_EARLY), :] = phase
        sum_ref[n * 8:(n + 1) * 8, :] += phase


def late_kernel(*refs):
    (early_ref, early_sum_ref), refs = refs[:2], refs[2:]
    blocks, (out_ref, sum_ref) = refs[:-2], refs[-2:]
    g, h = pl.program_id(0), pl.program_id(1)
    keys = [2, 3, 9, 10, 11, 12, "up", "down"]
    table = {key: (blocks[2 * i], blocks[2 * i + 1]) for i, key in enumerate(keys)}

    @pl.when(jnp.logical_and(g == 0, h == 0))
    def _():
        for l in range(LINES):
            for half in range(2):
                to = l * ROWS + half * PAD
                at = (l * 2 + half) * N_EARLY
                out_ref[to:to + N_EARLY, :] = early_ref[at:at + N_EARLY, :]
                out_ref[to + 48:to + PAD, :] = jnp.zeros((8, LANES), jnp.float32)
        sum_ref[:8 * N_EARLY, :] = early_sum_ref[...]
        sum_ref[8 * N_EARLY:, :] = jnp.zeros((8 * (PAD - N_EARLY), LANES), jnp.float32)

    def load(side, key, part, j):
        rows = pl.ds(j, 8, stride=8)
        if isinstance(key, tuple):
            return table[key[0]][side][key[1], part, rows, :]
        return table[key][side][0, part, rows, :]

    pairs = LATE + [(r, ("up", q - 13)) for r, q in AHEAD] + [(("down", r - 11), q - 13) for r, q in BACK]
    for n, phase in form(load, pairs):
        p = N_EARLY + n
        out_ref[pl.ds(g * (8 * ROWS) + h * PAD + p, 8, stride=ROWS), :] = phase
        sum_ref[p * 8:(p + 1) * 8, :] += phase

    @pl.when(jnp.logical_and(g == 1, h == 1))
    def _():
        owner = lax.axis_index("date")
        totals = jnp.sum(sum_ref[...], axis=1, keepdims=True)
        row = lax.broadcasted_iota(jnp.int32, (8 * PAD, LANES), 0) // 8
        lane = lax.broadcasted_iota(jnp.int32, (8 * PAD, LANES), 1)
        for i in range(DEPTH // LANES):
            hit = lane + i * LANES == owner * PAD + row
            line = jnp.sum(jnp.where(hit, totals, 0.0), axis=0, keepdims=True)
            for l in range(LINES):
                at = l * ROWS + (i // 4) * PAD + N_ALL + i % 4
                out_ref[at:at + 1, :] = line


def early_phases(slc):
    block = (DATES_DEV, 2, 64, LANES)
    return pl.pallas_call(
        early_kernel,
        grid=(2, 2),
        in_specs=[
            pl.BlockSpec(block, lambda g, h: (0, 0, g, 2 * h)),
            pl.BlockSpec(block, lambda g, h: (0, 0, g, 2 * h + 1)),
        ],
        out_specs=[
            pl.BlockSpec((LINES * 2 * N_EARLY, LANES), lambda g, h: (0, 0)),
            pl.BlockSpec((8 * N_EARLY, LANES), lambda g, h: (0, 0)),
        ],
        out_shape=[
            jax.ShapeDtypeStruct((LINES * 2 * N_EARLY, LANES), jnp.float32),
            jax.ShapeDtypeStruct((8 * N_EARLY, LANES), jnp.float32),
        ],
        compiler_params=pltpu.CompilerParams(vmem_limit_bytes=24 * 2**20),
        cost_estimate=pl.CostEstimate(flops=30_000_000, bytes_accessed=8_000_000, transcendentals=0),
        name="early_pairs",
    )(slc, slc)


def late_phases(early, early_sums, slc, up, down):
    def spec(depth, date, side):
        return pl.BlockSpec((depth, 2, 64, LANES), lambda g, h: (date, 0, g, 2 * h + side))

    arrays, specs = [], []
    for date in (2, 3, 9, 10, 11, 12):
        for side in range(2):
            arrays.append(slc)
            specs.append(spec(1, date, side))
    for array in (up, down):
        for side in range(2):
            arrays.append(array)
            specs.append(spec(2, 0, side))
    return pl.pallas_call(
        late_kernel,
        grid=(2, 2),
        in_specs=[
            pl.BlockSpec(early.shape, lambda g, h: (0, 0)),
            pl.BlockSpec(early_sums.shape, lambda g, h: (0, 0)),
        ] + specs,
        out_specs=pl.BlockSpec((LINES * ROWS, LANES), lambda g, h: (0, 0)),
        out_shape=jax.ShapeDtypeStruct((LINES * ROWS, LANES), jnp.float32),
        scratch_shapes=[pltpu.VMEM((8 * PAD, LANES), jnp.float32)],
        compiler_params=pltpu.CompilerParams(vmem_limit_bytes=24 * 2**20),
        cost_estimate=pl.CostEstimate(flops=10_000_000, bytes_accessed=6_000_000, transcendentals=0),
        name="late_pairs",
    )(early, early_sums, *arrays)


def series_kernel(x_ref, w_ref, sums_ref, out_ref):
    parts = []
    within = lax.broadcasted_iota(jnp.int32, (8, 256), 0)
    moved = jnp.logical_and(within >= 1, within < 4)
    for o in range(N):
        parts.append(w_ref[o * PAD:o * PAD + 48, :])
        before = (o + N - 1) % N * PAD
        parts.append(jnp.where(moved, w_ref[before + 48:before + PAD, :], w_ref[o * PAD + 48:(o + 1) * PAD, :]))
    weights = jnp.transpose(jnp.concatenate(parts, axis=0))[:TIMES]
    totals = jnp.zeros((TIMES, LANES), jnp.float32)
    for i in range(DEPTH // LANES):
        line = jnp.sum(sums_ref[:, i, :], axis=0, keepdims=True)
        totals += weights[:, i * LANES:(i + 1) * LANES] * line
    offset = jnp.sum(totals, axis=1, keepdims=True) * (1.0 / (LINES * 4096))
    lane = lax.broadcasted_iota(jnp.int32, (TIMES, LANES), 1)
    order = 2 * (lane % 64) + lane // 64
    for half in range(2):
        x = x_ref[:, half * PAD:(half + 1) * PAD, :].reshape(DEPTH, LANES)
        y = jnp.dot(weights, x, precision=lax.Precision.HIGHEST, preferred_element_type=jnp.float32)
        y = jnp.take_along_axis(y - offset, order, axis=1)
        out_ref[0, :, half * LANES:(half + 1) * LANES] = y[:207]


def series(x, w, sums):
    return pl.pallas_call(
        series_kernel,
        out_shape=jax.ShapeDtypeStruct((1, 207, 256), jnp.float32),
        compiler_params=pltpu.CompilerParams(vmem_limit_bytes=24 * 2**20),
        cost_estimate=pl.CostEstimate(flops=600_000_000, bytes_accessed=2_000_000, transcendentals=0),
        name="series",
    )(x, w, sums)


def per_device(slc, pair_slots, inversion):
    up = lax.ppermute(slc[:2], "date", [(i + 1, i) for i in range(N - 1)])
    down = lax.ppermute(slc[11:], "date", [(i, i + 1) for i in range(N - 1)])

    base = lax.axis_index("date") * DATES_DEV
    table = jnp.array(ORDER + [(-9, -9)] * (PAD - N_ALL), jnp.int32)
    local = jnp.where(pair_slots >= 0, pair_slots - base, -1)
    owned = (local[None, :, 0] == table[:, None, 0]) & (local[None, :, 1] == table[:, None, 1])
    w = jnp.dot(owned.astype(jnp.float32), jnp.pad(inversion, ((0, 256 - 207), (0, 0))).T,
                precision=lax.Precision.HIGHEST)
    w = lax.all_gather(w, "date", axis=0, tiled=True)

    early, early_sums = early_phases(slc)
    payload = late_phases(early, early_sums, slc, up, down)
    x = lax.all_to_all(payload.reshape(LINES, ROWS, LANES), "date", 0, 0, tiled=True)
    rows = jnp.sum(x, axis=0)
    rows = jnp.concatenate([rows[N_ALL:PAD], rows[PAD + N_ALL:]], axis=0)
    sums = lax.all_to_all(jnp.broadcast_to(rows, (N, 8, LANES)), "tile", 0, 0, tiled=True)
    return series(x, w, sums)


def solution(mesh):
    return jax.shard_map(
        per_device,
        mesh=mesh,
        in_specs=(P("date", None, None, "tile"), P("date", None), P(None, "date")),
        out_specs=P("date", None, "tile"),
        check_vma=False,
    )
```

```python
import jax
import jax.numpy as jnp
from jax import lax
from jax.experimental import pallas as pl
from jax.experimental.pallas import tpu as pltpu
from jax.sharding import PartitionSpec as P

N = 16
DATES_DEV = 13
SPAN = 4
LINES = 16
LANES = 128
CUT = 0.41421356

LATE = [(10, 12), (11, 12)]
AHEAD = [(9, 13), (10, 13), (10, 14), (11, 13), (11, 14), (12, 13), (12, 14)]
BACK = [(11, 15), (12, 15), (12, 16)]
EARLY = [
    (r, r + k)
    for r in range(DATES_DEV)
    for k in range(1, SPAN + 1)
    if r + k < DATES_DEV and (r, r + k) not in LATE
]
ORDER = EARLY + LATE + AHEAD + BACK
N_EARLY = len(EARLY)
N_ALL = len(ORDER)
PAD = 56
ROWS = 2 * PAD
DEPTH = N * PAD
TIMES = 208
VMEM = 32 * 2**20
HBM = pltpu.MemorySpace.HBM


def angle(re, im):
    size = jnp.abs(im)
    big = size > CUT * re
    num = jnp.where(big, size - re, size)
    den = jnp.where(big, size + re, re)
    t = num / den
    z = t * t
    p = ((8.05374449538e-2 * z - 1.38776856032e-1) * z + 1.99777106478e-1) * z - 3.33329491539e-1
    y = p * z * t + t
    y = jnp.where(big, y + 0.7853981633974483, y)
    y = jnp.where(im < 0, -y, y)
    return jnp.where(re > 0, y, 0.0)


def lane_iota():
    return lax.broadcasted_iota(jnp.int32, (8, LANES), 1)


def form(load, pairs):
    lane = lane_iota()
    even = (lane & 1) == 0
    swap = lane ^ 1
    by_ref = {}
    for n, (r, q) in enumerate(pairs):
        by_ref.setdefault(r, []).append((n, q))
    for r, members in by_ref.items():
        acc = {}
        for side in range(2):
            for j in range(8):
                a, b = load(side, r, 0, j), load(side, r, 1, j)
                for n, q in members:
                    c, d = load(side, q, 0, j), load(side, q, 1, j)
                    re = a * c + b * d
                    im = b * c - a * d
                    if j:
                        re = acc[n, side, 0] + re
                        im = acc[n, side, 1] + im
                    acc[n, side, 0], acc[n, side, 1] = re, im
        for n, _ in members:
            looked = []
            for part in range(2):
                left, right = acc[n, 0, part], acc[n, 1, part]
                kept = jnp.where(even, left, right)
                other = jnp.where(even, right, left)
                looked.append(kept + jnp.take_along_axis(other, swap, axis=1))
            yield n, angle(looked[0], looked[1])


def edges_kernel(slc_ref, head_ref, tail_ref, sems):
    copies = [
        pltpu.make_async_copy(slc_ref.at[:2], head_ref, sems.at[0]),
        pltpu.make_async_copy(slc_ref.at[11:], tail_ref, sems.at[1]),
    ]
    for copy in copies:
        copy.start()
    for copy in copies:
        copy.wait()


def edges(slc):
    edge = jax.ShapeDtypeStruct((2,) + slc.shape[1:], jnp.float32)
    anywhere = pl.BlockSpec(memory_space=pl.ANY)
    return pl.pallas_call(
        edges_kernel,
        in_specs=[pl.BlockSpec(memory_space=HBM)],
        out_specs=[anywhere, anywhere],
        out_shape=[edge, edge],
        scratch_shapes=[pltpu.SemaphoreType.DMA((2,))],
        compiler_params=pltpu.CompilerParams(vmem_limit_bytes=VMEM),
        cost_estimate=pl.CostEstimate(flops=0, bytes_accessed=4_000_000, transcendentals=0),
        name="edges",
    )(slc)


def order_kernel(slots_ref, inversion_ref, w_ref):
    base = lax.axis_index("date") * DATES_DEV
    first, second = slots_ref[:1, :], slots_ref[1:, :]
    code = jnp.where(first >= 0, (first - base) * 32 + (second - base), -1)
    row = lax.broadcasted_iota(jnp.int32, (PAD, 64), 0)
    wanted = jnp.full((PAD, 64), -2, jnp.int32)
    for p, (r, q) in enumerate(ORDER):
        wanted = jnp.where(row == p, r * 32 + q, wanted)
    own = jnp.where(wanted == code, 1.0, 0.0)
    w = jnp.dot(own, inversion_ref[...], precision=lax.Precision.HIGHEST, preferred_element_type=jnp.float32)
    w_ref[...] = jnp.zeros_like(w_ref)
    w_ref[:, :207] = w


def ordered_weights(pair_slots, inversion):
    return pl.pallas_call(
        order_kernel,
        out_shape=jax.ShapeDtypeStruct((PAD, 256), jnp.float32),
        compiler_params=pltpu.CompilerParams(vmem_limit_bytes=VMEM),
        cost_estimate=pl.CostEstimate(flops=10_000_000, bytes_accessed=100_000, transcendentals=0),
        name="ordered_weights",
    )(pair_slots.T, inversion.T)


def early_kernel(slc_ref, out_ref, sum_ref, data, stage, in_sems, out_sems):
    step = pl.program_id(0)
    g, h = step // 2, step % 2

    @pl.when(step == 0)
    def _():
        for s in range(4):
            for side in range(2):
                pltpu.make_async_copy(
                    slc_ref.at[:, :, pl.ds(s // 2 * 64, 64), pl.ds((s % 2 * 2 + side) * LANES, LANES)],
                    data.at[s, side], in_sems.at[s, side],
                ).start()
        sum_ref[...] = jnp.zeros_like(sum_ref)

    for side in range(2):
        pltpu.make_async_copy(
            slc_ref.at[:, :, pl.ds(0, 64), pl.ds(0, LANES)], data.at[step, side], in_sems.at[step, side]
        ).wait()

    def load(side, date, part, j):
        return data[step, side, date, part, pl.ds(j, 8, stride=8), :]

    for n, phase in form(load, EARLY):
        stage[pl.ds(g * (16 * N_EARLY) + h * N_EARLY + n, 8, stride=2 * N_EARLY), :] = phase
        sum_ref[n * 8:(n + 1) * 8, :] += phase

    def out_copy(half):
        return pltpu.make_async_copy(
            stage.reshape(2 * LINES, N_EARLY, LANES).at[pl.ds(half * LINES, LINES)],
            out_ref.at[pl.ds(half * LINES, LINES), pl.ds(0, N_EARLY), :], out_sems.at[half],
        )

    @pl.when(step == 1)
    def _():
        out_copy(0).start()

    @pl.when(step == 3)
    def _():
        out_copy(1).start()
        out_copy(0).wait()
        out_copy(1).wait()


def late_kernel(slc_ref, up_ref, down_ref, early_sum_ref, early_ref, out_ref, data, stage, sum_ref, in_sems, out_sem):
    del early_ref
    step = pl.program_id(0)
    h, g = step // 2, step % 2

    def copies(at):
        columns = pl.ds(at * LANES, LANES)
        return [
            pltpu.make_async_copy(slc_ref.at[9:13, :, :, columns], data.at[at, 0:4], in_sems.at[at, 0]),
            pltpu.make_async_copy(slc_ref.at[2:4, :, :, columns], data.at[at, 4:6], in_sems.at[at, 1]),
            pltpu.make_async_copy(up_ref.at[:, :, :, columns], data.at[at, 6:8], in_sems.at[at, 2]),
            pltpu.make_async_copy(down_ref.at[:, :, :, columns], data.at[at, 8:10], in_sems.at[at, 3]),
        ]

    @pl.when(step == 0)
    def _():
        for at in range(4):
            for copy in copies(at):
                copy.start()
        sum_ref[...] = jnp.zeros_like(sum_ref)

    for half in range(2):
        @pl.when(step == 2 * half)
        def _():
            for at in (2 * half, 2 * half + 1):
                for copy in copies(at):
                    copy.wait()

    slot = {9: 0, 10: 1, 11: 2, 12: 3, 2: 4, 3: 5, 13: 6, 14: 7, -2: 8, -1: 9}

    def load(side, date, part, j):
        return data[h * 2 + side, slot[date], part, pl.ds(g * 64 + j, 8, stride=8), :]

    pairs = LATE + AHEAD + [(r - DATES_DEV, q - DATES_DEV) for r, q in BACK]
    for n, phase in form(load, pairs):
        stage[pl.ds(g * 256 + h * 16 + n, 8, stride=32), :] = phase
        sum_ref[n * 8:(n + 1) * 8, :] += phase

    @pl.when(step == 3)
    def _():
        owner = lax.axis_index("date")
        lines = [jnp.zeros((1, LANES), jnp.float32) for _ in range(8)]
        for first, ref in ((0, early_sum_ref), (N_EARLY, sum_ref)):
            totals = jnp.sum(ref[...], axis=1, keepdims=True)
            row = lax.broadcasted_iota(jnp.int32, ref.shape, 0) // 8 + first + owner * PAD
            lane = lax.broadcasted_iota(jnp.int32, ref.shape, 1)
            for i in range(DEPTH // LANES):
                hit = lane + i * LANES == row
                lines[i] += jnp.sum(jnp.where(hit, totals, 0.0), axis=0, keepdims=True)
        for half in range(2):
            four = jnp.concatenate(lines[4 * half:4 * half + 4], axis=0)
            for l in range(LINES):
                at = (l * 2 + half) * 16 + 12
                stage[at:at + 4, :] = four
        copy = pltpu.make_async_copy(
            stage.reshape(2 * LINES, 16, LANES), out_ref.at[:, pl.ds(N_EARLY, 16), :], out_sem
        )
        copy.start()
        copy.wait()


def early_phases(slc):
    return pl.pallas_call(
        early_kernel,
        grid=(4,),
        in_specs=[pl.BlockSpec(memory_space=HBM)],
        out_specs=[
            pl.BlockSpec(memory_space=pl.ANY),
            pl.BlockSpec((8 * N_EARLY, LANES), lambda i: (0, 0)),
        ],
        out_shape=[
            jax.ShapeDtypeStruct((2 * LINES, PAD, LANES), jnp.float32),
            jax.ShapeDtypeStruct((8 * N_EARLY, LANES), jnp.float32),
        ],
        scratch_shapes=[
            pltpu.VMEM((4, 2, DATES_DEV, 2, 64, LANES), jnp.float32),
            pltpu.VMEM((2 * LINES * N_EARLY, LANES), jnp.float32),
            pltpu.SemaphoreType.DMA((4, 2)),
            pltpu.SemaphoreType.DMA((2,)),
        ],
        compiler_params=pltpu.CompilerParams(vmem_limit_bytes=VMEM),
        cost_estimate=pl.CostEstimate(flops=30_000_000, bytes_accessed=8_000_000, transcendentals=0),
        name="early_pairs",
    )(slc)


def late_phases(early, early_sums, slc, up, down):
    anywhere = pl.BlockSpec(memory_space=pl.ANY)
    return pl.pallas_call(
        late_kernel,
        grid=(4,),
        in_specs=[
            pl.BlockSpec(memory_space=HBM), anywhere, anywhere,
            pl.BlockSpec(early_sums.shape, lambda i: (0, 0)), anywhere,
        ],
        out_specs=anywhere,
        out_shape=jax.ShapeDtypeStruct(early.shape, jnp.float32),
        input_output_aliases={4: 0},
        scratch_shapes=[
            pltpu.VMEM((4, 10, 2, 128, LANES), jnp.float32),
            pltpu.VMEM((2 * LINES * 16, LANES), jnp.float32),
            pltpu.VMEM((8 * 16, LANES), jnp.float32),
            pltpu.SemaphoreType.DMA((4, 4)),
            pltpu.SemaphoreType.DMA,
        ],
        compiler_params=pltpu.CompilerParams(vmem_limit_bytes=VMEM),
        cost_estimate=pl.CostEstimate(flops=10_000_000, bytes_accessed=6_000_000, transcendentals=0),
        name="late_pairs",
    )(slc, up, down, early_sums, early)


def product_kernel(x_ref, w_ref, out_ref, weights_ref):
    device = lax.axis_index("date")
    within = lax.broadcasted_iota(jnp.int32, (8, 256), 0)
    moved = jnp.logical_and(within >= 1, within < 4)
    parts = []
    for o in range(N):
        here = w_ref.at[(o - device) & (N - 1)]
        before = w_ref.at[(o - 1 - device) & (N - 1)]
        parts.append(here[:48, :])
        parts.append(jnp.where(moved, before[48:, :], here[48:, :]))
    weights = jnp.transpose(jnp.concatenate(parts, axis=0))[:TIMES]
    weights_ref[...] = weights
    lane = lax.broadcasted_iota(jnp.int32, (TIMES, LANES), 1)
    order = 2 * (lane % 64) + lane // 64
    for half in range(2):
        x = x_ref[:, half * PAD:(half + 1) * PAD, :].reshape(DEPTH, LANES)
        y = jnp.dot(weights, x, precision=lax.Precision.HIGHEST, preferred_element_type=jnp.float32)
        out_ref[:, half * LANES:(half + 1) * LANES] = jnp.take_along_axis(y, order, axis=1)


def product(x, w):
    return pl.pallas_call(
        product_kernel,
        out_shape=[
            jax.ShapeDtypeStruct((TIMES, 256), jnp.float32),
            jax.ShapeDtypeStruct((TIMES, DEPTH), jnp.float32),
        ],
        compiler_params=pltpu.CompilerParams(vmem_limit_bytes=VMEM),
        cost_estimate=pl.CostEstimate(flops=600_000_000, bytes_accessed=2_000_000, transcendentals=0),
        name="product",
    )(x, w)


def centre_kernel(y_ref, weights_ref, sums_ref, out_ref):
    totals = jnp.zeros((TIMES, LANES), jnp.float32)
    for i in range(DEPTH // LANES):
        line = jnp.sum(sums_ref[:, i, :], axis=0, keepdims=True)
        totals += weights_ref[:, i * LANES:(i + 1) * LANES] * line
    offset = jnp.sum(totals, axis=1, keepdims=True) * (1.0 / (LINES * 4096))
    out_ref[:, 0, :] = (y_ref[...] - offset)[:207]


def centre(y, weights, sums):
    return pl.pallas_call(
        centre_kernel,
        out_shape=jax.ShapeDtypeStruct((207, 1, 256), jnp.float32),
        compiler_params=pltpu.CompilerParams(vmem_limit_bytes=VMEM),
        cost_estimate=pl.CostEstimate(flops=400_000, bytes_accessed=1_200_000, transcendentals=0),
        name="centre",
    )(y, weights, sums)


def per_device(slc, pair_slots, inversion):
    slc = pltpu.with_memory_space_constraint(slc, HBM)
    head, tail = edges(slc)
    up = lax.ppermute(head, "date", [(i + 1, i) for i in range(N - 1)])
    down = lax.ppermute(tail, "date", [(i, i + 1) for i in range(N - 1)])
    early, early_sums = early_phases(slc)
    pair_slots, inversion, early_sums = lax.optimization_barrier((pair_slots, inversion, early_sums))
    w = ordered_weights(pair_slots, inversion)
    w = lax.ppermute(w, ("date", "tile"), [(o * N + j, (o - j) % N * N + j) for o in range(N) for j in range(N)])

    payload = late_phases(early, early_sums, slc, up, down)
    w, payload = lax.optimization_barrier((w, payload))
    x = lax.all_to_all(payload.reshape(LINES, ROWS, LANES), "date", 0, 0, tiled=True)
    w = lax.all_gather(w, "tile", axis=0)
    rows = jnp.sum(x, axis=0)
    rows = jnp.concatenate([rows[N_ALL:PAD], rows[PAD + N_ALL:]], axis=0)
    rows, w = lax.optimization_barrier((rows, w))
    sums = lax.all_to_all(jnp.broadcast_to(rows, (N, 8, LANES)), "tile", 0, 0, tiled=True)
    return jnp.swapaxes(centre(*product(x, w), sums), 0, 1)


def solution(mesh):
    return jax.shard_map(
        per_device,
        mesh=mesh,
        in_specs=(P("date", None, None, "tile"), P("date", None), P(None, "date")),
        out_specs=P("date", None, "tile"),
        check_vma=False,
    )
```

```python
import jax
import jax.numpy as jnp
from jax import lax
from jax.experimental import pallas as pl
from jax.experimental.pallas import tpu as pltpu
from jax.sharding import PartitionSpec as P

N = 16
DATES_DEV = 13
SPAN = 4
LINES = 16
LANES = 128
CUT = 0.41421356

LATE = [(10, 12), (11, 12)]
AHEAD = [(9, 13), (10, 13), (10, 14), (11, 13), (11, 14), (12, 13), (12, 14)]
BACK = [(11, 15), (12, 15), (12, 16)]
EARLY = [
    (r, r + k)
    for r in range(DATES_DEV)
    for k in range(1, SPAN + 1)
    if r + k < DATES_DEV and (r, r + k) not in LATE
]
ORDER = EARLY + LATE + AHEAD + BACK
N_EARLY = len(EARLY)
N_ALL = len(ORDER)
PAD = 56
ROWS = 2 * PAD
DEPTH = N * PAD
TIMES = 208
VMEM = 32 * 2**20
BLOCK = 4
HBM = pltpu.MemorySpace.HBM


def angle(re, im):
    size = jnp.abs(im)
    big = size > CUT * re
    num = jnp.where(big, size - re, size)
    den = jnp.where(big, size + re, re)
    t = num / den
    z = t * t
    p = ((8.05374449538e-2 * z - 1.38776856032e-1) * z + 1.99777106478e-1) * z - 3.33329491539e-1
    y = p * z * t + t
    y = jnp.where(big, y + 0.7853981633974483, y)
    y = jnp.where(im < 0, -y, y)
    return jnp.where(re > 0, y, 0.0)


def lane_iota():
    return lax.broadcasted_iota(jnp.int32, (8, LANES), 1)


def form(load, blocks):
    lane = lane_iota()
    even = (lane & 1) == 0
    swap = lane ^ 1
    for block in blocks:
        acc = {}
        for side in range(2):
            for j in range(8):
                held = {key: (load(side, key, 0, j), load(side, key, 1, j)) for key in {k: 0 for n, r, q in block for k in (r, q)}}
                for n, r, q in block:
                    (a, b), (c, d) = held[r], held[q]
                    re = a * c + b * d
                    im = b * c - a * d
                    if j:
                        re = acc[n, side, 0] + re
                        im = acc[n, side, 1] + im
                    acc[n, side, 0], acc[n, side, 1] = re, im
        for n, _, _ in block:
            looked = []
            for part in range(2):
                left, right = acc[n, 0, part], acc[n, 1, part]
                kept = jnp.where(even, left, right)
                other = jnp.where(even, right, left)
                looked.append(kept + jnp.take_along_axis(other, swap, axis=1))
            yield n, angle(looked[0], looked[1])


def blocks_of(pairs, groups):
    numbered = [(n, r, q) for n, (r, q) in enumerate(pairs)]
    return [[entry for entry in numbered if entry[1] in group] for group in groups]


def edges_kernel(slc_ref, head_ref, tail_ref, sems):
    copies = []
    for c in range(4):
        columns = pl.ds(c * LANES, LANES)
        copies.append(pltpu.make_async_copy(slc_ref.at[0:2, :, :, columns], head_ref.at[c], sems.at[0, c]))
        copies.append(pltpu.make_async_copy(slc_ref.at[11:13, :, :, columns], tail_ref.at[c], sems.at[1, c]))
    for copy in copies:
        copy.start()
    for copy in copies:
        copy.wait()


def edges(slc):
    edge = jax.ShapeDtypeStruct((4, 2, 2, 128, LANES), jnp.float32)
    vmem = pl.BlockSpec(memory_space=pltpu.VMEM)
    return pl.pallas_call(
        edges_kernel,
        in_specs=[pl.BlockSpec(memory_space=HBM)],
        out_specs=[vmem, vmem],
        out_shape=[edge, edge],
        scratch_shapes=[pltpu.SemaphoreType.DMA((2, 4))],
        compiler_params=pltpu.CompilerParams(vmem_limit_bytes=VMEM),
        cost_estimate=pl.CostEstimate(flops=0, bytes_accessed=4_000_000, transcendentals=0),
        name="edges",
    )(slc)


def order_kernel(slots_ref, inversion_ref, w_ref):
    base = lax.axis_index("date") * DATES_DEV
    first, second = slots_ref[:1, :], slots_ref[1:, :]
    code = jnp.where(first >= 0, (first - base) * 32 + (second - base), -1)
    row = lax.broadcasted_iota(jnp.int32, (PAD, 64), 0)
    wanted = jnp.full((PAD, 64), -2, jnp.int32)
    for p, (r, q) in enumerate(ORDER):
        wanted = jnp.where(row == p, r * 32 + q, wanted)
    own = jnp.where(wanted == code, 1.0, 0.0)
    w = jnp.dot(own, inversion_ref[...], precision=lax.Precision.HIGHEST, preferred_element_type=jnp.float32)
    w_ref[...] = jnp.zeros_like(w_ref)
    w_ref[:, :207] = w


def ordered_weights(pair_slots, inversion):
    return pl.pallas_call(
        order_kernel,
        out_shape=jax.ShapeDtypeStruct((PAD, 256), jnp.float32),
        compiler_params=pltpu.CompilerParams(vmem_limit_bytes=VMEM),
        cost_estimate=pl.CostEstimate(flops=10_000_000, bytes_accessed=100_000, transcendentals=0),
        name="ordered_weights",
    )(pair_slots.T, inversion.T)


def early_kernel(slc_ref, out_ref, sum_ref, keep_ref, data, stage, in_sems, out_sems, keep_sems):
    step = pl.program_id(0)
    g, h = step // 2, step % 2

    def copies(s):
        rows = pl.ds(s // 2 * 64, 64)
        return [
            pltpu.make_async_copy(
                slc_ref.at[:, :, rows, pl.ds((s % 2 * 2 + side) * LANES, LANES)], data.at[s, side], in_sems.at[s, side]
            )
            for side in range(2)
        ]

    @pl.when(step == 0)
    def _():
        for copy in copies(0):
            copy.start()
        sum_ref[...] = jnp.zeros_like(sum_ref)

    for s in range(4):
        @pl.when(step == s)
        def _():
            for copy in copies(s):
                copy.wait()
            for later in ((1, 2) if s == 0 else (s + 2,)):
                if later < 4:
                    for copy in copies(later):
                        copy.start()

    def kept(c):
        columns = pl.ds(c * LANES, LANES)
        return [
            pltpu.make_async_copy(slc_ref.at[9:13, :, :, columns], keep_ref.at[c, 0:4], keep_sems.at[c, 0]),
            pltpu.make_async_copy(slc_ref.at[2:4, :, :, columns], keep_ref.at[c, 4:6], keep_sems.at[c, 1]),
        ]

    @pl.when(step == 2)
    def _():
        for c in range(4):
            for copy in kept(c):
                copy.start()

    def load(side, date, part, j):
        return data[step, side, date, part, pl.ds(j, 8, stride=8), :]

    groups = [range(r, r + BLOCK) for r in range(0, DATES_DEV, BLOCK)]
    for n, phase in form(load, blocks_of(EARLY, groups)):
        stage[pl.ds(g * (16 * N_EARLY) + h * N_EARLY + n, 8, stride=2 * N_EARLY), :] = phase
        sum_ref[n * 8:(n + 1) * 8, :] += phase

    def out_copy(half):
        return pltpu.make_async_copy(
            stage.reshape(2 * LINES, N_EARLY, LANES).at[pl.ds(half * LINES, LINES)],
            out_ref.at[pl.ds(half * LINES, LINES), pl.ds(0, N_EARLY), :], out_sems.at[half],
        )

    @pl.when(step == 1)
    def _():
        out_copy(0).start()

    @pl.when(step == 3)
    def _():
        out_copy(1).start()
        for c in range(4):
            for copy in kept(c):
                copy.wait()
        out_copy(0).wait()
        out_copy(1).wait()


def late_kernel(keep_ref, up_ref, down_ref, early_sum_ref, early_ref, out_ref, stage, sum_ref, total_ref, out_sem):
    del early_ref
    step = pl.program_id(0)
    h, g = step // 2, step % 2

    @pl.when(step == 0)
    def _():
        sum_ref[...] = jnp.zeros_like(sum_ref)

    slot = {9: (keep_ref, 0), 10: (keep_ref, 1), 11: (keep_ref, 2), 12: (keep_ref, 3), 2: (keep_ref, 4),
            3: (keep_ref, 5), 13: (up_ref, 0), 14: (up_ref, 1), -2: (down_ref, 0), -1: (down_ref, 1)}

    def load(side, date, part, j):
        ref, at = slot[date]
        return ref[h * 2 + side, at, part, pl.ds(g * 64 + j, 8, stride=8), :]

    pairs = LATE + AHEAD + [(r - DATES_DEV, q - DATES_DEV) for r, q in BACK]
    for n, phase in form(load, blocks_of(pairs, [(9, 10, 11, 12), (-2, -1)])):
        stage[pl.ds(g * 256 + h * 16 + n, 8, stride=32), :] = phase
        sum_ref[n * 8:(n + 1) * 8, :] += phase

    @pl.when(step == 3)
    def _():
        total_ref[N_ALL:, :] = jnp.zeros((PAD - N_ALL, LANES), jnp.float32)
        for first, ref in ((0, early_sum_ref), (N_EARLY, sum_ref)):
            count = ref.shape[0] // 8
            total = jnp.sum(jnp.sum(ref[...].reshape(count, 8, LANES), axis=1), axis=1, keepdims=True)
            total_ref[first:first + count, :] = jnp.broadcast_to(total, (count, LANES))
        row = lax.broadcasted_iota(jnp.int32, (PAD, LANES), 0) + lax.axis_index("date") * PAD
        lane = lax.broadcasted_iota(jnp.int32, (PAD, LANES), 1)
        total = total_ref[...]
        lines = [
            jnp.sum(jnp.where(lane + i * LANES == row, total, 0.0), axis=0, keepdims=True) for i in range(8)
        ]
        for half in range(2):
            four = jnp.concatenate(lines[4 * half:4 * half + 4], axis=0)
            for l in range(LINES):
                at = (l * 2 + half) * 16 + 12
                stage[at:at + 4, :] = four
        copy = pltpu.make_async_copy(
            stage.reshape(2 * LINES, 16, LANES), out_ref.at[:, pl.ds(N_EARLY, 16), :], out_sem
        )
        copy.start()
        copy.wait()


def early_phases(slc):
    return pl.pallas_call(
        early_kernel,
        grid=(4,),
        in_specs=[pl.BlockSpec(memory_space=HBM)],
        out_specs=[
            pl.BlockSpec(memory_space=pl.ANY),
            pl.BlockSpec((8 * N_EARLY, LANES), lambda i: (0, 0)),
            pl.BlockSpec(memory_space=pltpu.VMEM),
        ],
        out_shape=[
            jax.ShapeDtypeStruct((2 * LINES, PAD, LANES), jnp.float32),
            jax.ShapeDtypeStruct((8 * N_EARLY, LANES), jnp.float32),
            jax.ShapeDtypeStruct((4, 6, 2, 128, LANES), jnp.float32),
        ],
        scratch_shapes=[
            pltpu.VMEM((4, 2, DATES_DEV, 2, 64, LANES), jnp.float32),
            pltpu.VMEM((2 * LINES * N_EARLY, LANES), jnp.float32),
            pltpu.SemaphoreType.DMA((4, 2)),
            pltpu.SemaphoreType.DMA((2,)),
            pltpu.SemaphoreType.DMA((4, 2)),
        ],
        compiler_params=pltpu.CompilerParams(vmem_limit_bytes=VMEM),
        cost_estimate=pl.CostEstimate(flops=30_000_000, bytes_accessed=8_000_000, transcendentals=0),
        name="early_pairs",
    )(slc)


def late_phases(early, early_sums, keep, up, down):
    anywhere = pl.BlockSpec(memory_space=pl.ANY)
    vmem = pl.BlockSpec(memory_space=pltpu.VMEM)
    return pl.pallas_call(
        late_kernel,
        grid=(4,),
        in_specs=[vmem, vmem, vmem, vmem, anywhere],
        out_specs=anywhere,
        out_shape=jax.ShapeDtypeStruct(early.shape, jnp.float32),
        input_output_aliases={4: 0},
        scratch_shapes=[
            pltpu.VMEM((2 * LINES * 16, LANES), jnp.float32),
            pltpu.VMEM((8 * 16, LANES), jnp.float32),
            pltpu.VMEM((PAD, LANES), jnp.float32),
            pltpu.SemaphoreType.DMA,
        ],
        compiler_params=pltpu.CompilerParams(vmem_limit_bytes=VMEM),
        cost_estimate=pl.CostEstimate(flops=10_000_000, bytes_accessed=6_000_000, transcendentals=0),
        name="late_pairs",
    )(keep, up, down, early_sums, early)


def spread_kernel(x_ref, out_ref):
    rows = [jnp.sum(x_ref[:, at + 48:at + PAD, :], axis=0)[4:] for at in (0, PAD)]
    out_ref[...] = jnp.broadcast_to(jnp.concatenate(rows, axis=0)[None], (N, 8, LANES))


def spread(x):
    return pl.pallas_call(
        spread_kernel,
        out_shape=jax.ShapeDtypeStruct((N, 8, LANES), jnp.float32),
        compiler_params=pltpu.CompilerParams(vmem_limit_bytes=VMEM),
        cost_estimate=pl.CostEstimate(flops=100_000, bytes_accessed=1_000_000, transcendentals=0),
        name="spread",
    )(x)


def product_kernel(x_ref, w_ref, out_ref, weights_ref):
    device = lax.axis_index("date")
    within = lax.broadcasted_iota(jnp.int32, (8, 256), 0)
    moved = jnp.logical_and(within >= 1, within < 4)
    parts = []
    for o in range(N):
        here = w_ref.at[(o - device) & (N - 1)]
        before = w_ref.at[(o - 1 - device) & (N - 1)]
        parts.append(here[:48, :])
        parts.append(jnp.where(moved, before[48:, :], here[48:, :]))
    weights = jnp.transpose(jnp.concatenate(parts, axis=0))[:TIMES]
    weights_ref[...] = weights
    lane = lax.broadcasted_iota(jnp.int32, (TIMES, LANES), 1)
    order = 2 * (lane % 64) + lane // 64
    for half in range(2):
        x = x_ref[:, half * PAD:(half + 1) * PAD, :].reshape(DEPTH, LANES)
        y = jnp.dot(weights, x, precision=lax.Precision.HIGHEST, preferred_element_type=jnp.float32)
        out_ref[:, half * LANES:(half + 1) * LANES] = jnp.take_along_axis(y, order, axis=1)


def product(x, w):
    return pl.pallas_call(
        product_kernel,
        out_shape=[
            jax.ShapeDtypeStruct((TIMES, 256), jnp.float32),
            jax.ShapeDtypeStruct((TIMES, DEPTH), jnp.float32),
        ],
        compiler_params=pltpu.CompilerParams(vmem_limit_bytes=VMEM),
        cost_estimate=pl.CostEstimate(flops=600_000_000, bytes_accessed=2_000_000, transcendentals=0),
        name="product",
    )(x, w)


def centre_kernel(y_ref, weights_ref, sums_ref, out_ref):
    totals = jnp.zeros((TIMES, LANES), jnp.float32)
    for i in range(DEPTH // LANES):
        line = jnp.sum(sums_ref[:, i, :], axis=0, keepdims=True)
        totals += weights_ref[:, i * LANES:(i + 1) * LANES] * line
    offset = jnp.sum(totals, axis=1, keepdims=True) * (1.0 / (LINES * 4096))
    out_ref[:, 0, :] = (y_ref[...] - offset)[:207]


def centre(y, weights, sums):
    return pl.pallas_call(
        centre_kernel,
        out_shape=jax.ShapeDtypeStruct((207, 1, 256), jnp.float32),
        compiler_params=pltpu.CompilerParams(vmem_limit_bytes=VMEM),
        cost_estimate=pl.CostEstimate(flops=400_000, bytes_accessed=1_200_000, transcendentals=0),
        name="centre",
    )(y, weights, sums)


def per_device(slc, pair_slots, inversion):
    slc = pltpu.with_memory_space_constraint(slc, HBM)
    head, tail = edges(slc)
    up = lax.ppermute(head, "date", [(i + 1, i) for i in range(N - 1)])
    down = lax.ppermute(tail, "date", [(i, i + 1) for i in range(N - 1)])
    early, early_sums, keep = early_phases(slc)
    pair_slots, inversion, early_sums = lax.optimization_barrier((pair_slots, inversion, early_sums))
    w = ordered_weights(pair_slots, inversion)
    w = lax.ppermute(w, ("date", "tile"), [(o * N + j, (o - j) % N * N + j) for o in range(N) for j in range(N)])

    payload = late_phases(early, early_sums, keep, up, down)
    w, payload = lax.optimization_barrier((w, payload))
    x = lax.all_to_all(payload.reshape(LINES, ROWS, LANES), "date", 0, 0, tiled=True)
    w = lax.all_gather(w, "tile", axis=0)
    rows, w = lax.optimization_barrier((spread(x), w))
    sums = lax.all_to_all(rows, "tile", 0, 0, tiled=True)
    return jnp.swapaxes(centre(*product(x, w), sums), 0, 1)


def solution(mesh):
    return jax.shard_map(
        per_device,
        mesh=mesh,
        in_specs=(P("date", None, None, "tile"), P("date", None), P(None, "date")),
        out_specs=P("date", None, "tile"),
        check_vma=False,
    )
```

```python
import jax
import jax.numpy as jnp
from jax import lax
from jax.experimental import pallas as pl
from jax.experimental.pallas import tpu as pltpu
from jax.sharding import PartitionSpec as P

N = 16
DATES_DEV = 13
SPAN = 4
LINES = 16
LANES = 128
CUT = 0.41421356

LATE = [(10, 12), (11, 12)]
AHEAD = [(9, 13), (10, 13), (10, 14), (11, 13), (11, 14), (12, 13), (12, 14)]
BACK = [(11, 15), (12, 15), (12, 16)]
EARLY = [
    (r, r + k)
    for r in range(DATES_DEV)
    for k in range(1, SPAN + 1)
    if r + k < DATES_DEV and (r, r + k) not in LATE
]
ORDER = EARLY + LATE + AHEAD + BACK
N_EARLY = len(EARLY)
N_ALL = len(ORDER)
PAD = 56
ROWS = 2 * PAD
DEPTH = N * PAD
TIMES = 208
VMEM = 32 * 2**20
BLOCK = 4
HBM = pltpu.MemorySpace.HBM


def angle(re, im):
    size = jnp.abs(im)
    big = size > CUT * re
    num = jnp.where(big, size - re, size)
    den = jnp.where(big, size + re, re)
    t = num / den
    z = t * t
    p = ((8.05374449538e-2 * z - 1.38776856032e-1) * z + 1.99777106478e-1) * z - 3.33329491539e-1
    y = p * z * t + t
    y = jnp.where(big, y + 0.7853981633974483, y)
    y = jnp.where(im < 0, -y, y)
    return jnp.where(re > 0, y, 0.0)


def lane_iota():
    return lax.broadcasted_iota(jnp.int32, (8, LANES), 1)


def form(load, blocks):
    lane = lane_iota()
    even = (lane & 1) == 0
    swap = lane ^ 1
    for block in blocks:
        acc = {}
        for side in range(2):
            for j in range(8):
                held = {key: (load(side, key, 0, j), load(side, key, 1, j)) for key in {k: 0 for n, r, q in block for k in (r, q)}}
                for n, r, q in block:
                    (a, b), (c, d) = held[r], held[q]
                    re = a * c + b * d
                    im = b * c - a * d
                    if j:
                        re = acc[n, side, 0] + re
                        im = acc[n, side, 1] + im
                    acc[n, side, 0], acc[n, side, 1] = re, im
        for n, _, _ in block:
            looked = []
            for part in range(2):
                left, right = acc[n, 0, part], acc[n, 1, part]
                kept = jnp.where(even, left, right)
                other = jnp.where(even, right, left)
                looked.append(kept + jnp.take_along_axis(other, swap, axis=1))
            yield n, angle(looked[0], looked[1])


def blocks_of(pairs, groups):
    numbered = [(n, r, q) for n, (r, q) in enumerate(pairs)]
    return [[entry for entry in numbered if entry[1] in group] for group in groups]


def edges_kernel(slc_ref, head_ref, tail_ref, sems):
    copies = []
    for c in range(4):
        columns = pl.ds(c * LANES, LANES)
        copies.append(pltpu.make_async_copy(slc_ref.at[0:2, :, :, columns], head_ref.at[c], sems.at[0, c]))
        copies.append(pltpu.make_async_copy(slc_ref.at[11:13, :, :, columns], tail_ref.at[c], sems.at[1, c]))
    for copy in copies:
        copy.start()
    for copy in copies:
        copy.wait()


def edges(slc):
    edge = jax.ShapeDtypeStruct((4, 2, 2, 128, LANES), jnp.float32)
    vmem = pl.BlockSpec(memory_space=pltpu.VMEM)
    return pl.pallas_call(
        edges_kernel,
        in_specs=[pl.BlockSpec(memory_space=HBM)],
        out_specs=[vmem, vmem],
        out_shape=[edge, edge],
        scratch_shapes=[pltpu.SemaphoreType.DMA((2, 4))],
        compiler_params=pltpu.CompilerParams(vmem_limit_bytes=VMEM),
        cost_estimate=pl.CostEstimate(flops=0, bytes_accessed=4_000_000, transcendentals=0),
        name="edges",
    )(slc)


def order_kernel(slots_ref, inversion_ref, w_ref):
    base = lax.axis_index("date") * DATES_DEV
    first, second = slots_ref[:1, :], slots_ref[1:, :]
    code = jnp.where(first >= 0, (first - base) * 32 + (second - base), -1)
    row = lax.broadcasted_iota(jnp.int32, (PAD, 64), 0)
    wanted = jnp.full((PAD, 64), -2, jnp.int32)
    for p, (r, q) in enumerate(ORDER):
        wanted = jnp.where(row == p, r * 32 + q, wanted)
    own = jnp.where(wanted == code, 1.0, 0.0)
    w = jnp.dot(own, inversion_ref[...], precision=lax.Precision.HIGHEST, preferred_element_type=jnp.float32)
    w_ref[...] = jnp.zeros_like(w_ref)
    w_ref[:, :207] = w


def ordered_weights(pair_slots, inversion):
    return pl.pallas_call(
        order_kernel,
        out_shape=jax.ShapeDtypeStruct((PAD, 256), jnp.float32),
        compiler_params=pltpu.CompilerParams(vmem_limit_bytes=VMEM),
        cost_estimate=pl.CostEstimate(flops=10_000_000, bytes_accessed=100_000, transcendentals=0),
        name="ordered_weights",
    )(pair_slots.T, inversion.T)


def early_kernel(slc_ref, out_ref, sum_ref, keep_ref, data, stage, in_sems, out_sems, keep_sems):
    step = pl.program_id(0)
    g, h = step // 2, step % 2

    def copies(s):
        rows = pl.ds(s // 2 * 64, 64)
        return [
            pltpu.make_async_copy(
                slc_ref.at[:, :, rows, pl.ds((s % 2 * 2 + side) * LANES, LANES)], data.at[s, side], in_sems.at[s, side]
            )
            for side in range(2)
        ]

    @pl.when(step == 0)
    def _():
        for copy in copies(0) + copies(1):
            copy.start()
        sum_ref[...] = jnp.zeros_like(sum_ref)

    for s in range(4):
        @pl.when(step == s)
        def _():
            for copy in copies(s):
                copy.wait()
            for later in (s + 2,):
                if later < 4:
                    for copy in copies(later):
                        copy.start()

    def kept(c):
        columns = pl.ds(c * LANES, LANES)
        return [
            pltpu.make_async_copy(slc_ref.at[9:13, :, :, columns], keep_ref.at[c, 0:4], keep_sems.at[c, 0]),
            pltpu.make_async_copy(slc_ref.at[2:4, :, :, columns], keep_ref.at[c, 4:6], keep_sems.at[c, 1]),
        ]

    @pl.when(step == 2)
    def _():
        for c in range(4):
            for copy in kept(c):
                copy.start()

    def load(side, date, part, j):
        return data[step, side, date, part, pl.ds(j, 8, stride=8), :]

    groups = [range(r, r + BLOCK) for r in range(0, DATES_DEV, BLOCK)]
    for n, phase in form(load, blocks_of(EARLY, groups)):
        stage[pl.ds(g * (16 * N_EARLY) + h * N_EARLY + n, 8, stride=2 * N_EARLY), :] = phase
        sum_ref[n * 8:(n + 1) * 8, :] += phase

    def out_copy(half):
        return pltpu.make_async_copy(
            stage.reshape(2 * LINES, N_EARLY, LANES).at[pl.ds(half * LINES, LINES)],
            out_ref.at[pl.ds(half * LINES, LINES), pl.ds(0, N_EARLY), :], out_sems.at[half],
        )

    @pl.when(step == 1)
    def _():
        out_copy(0).start()

    @pl.when(step == 3)
    def _():
        out_copy(1).start()
        for c in range(4):
            for copy in kept(c):
                copy.wait()
        out_copy(0).wait()
        out_copy(1).wait()


def late_kernel(keep_ref, up_ref, down_ref, early_sum_ref, early_ref, out_ref, stage, sum_ref, total_ref, out_sem):
    del early_ref
    step = pl.program_id(0)
    h, g = step // 2, step % 2

    @pl.when(step == 0)
    def _():
        sum_ref[...] = jnp.zeros_like(sum_ref)

    slot = {9: (keep_ref, 0), 10: (keep_ref, 1), 11: (keep_ref, 2), 12: (keep_ref, 3), 2: (keep_ref, 4),
            3: (keep_ref, 5), 13: (up_ref, 0), 14: (up_ref, 1), -2: (down_ref, 0), -1: (down_ref, 1)}

    def load(side, date, part, j):
        ref, at = slot[date]
        return ref[h * 2 + side, at, part, pl.ds(g * 64 + j, 8, stride=8), :]

    pairs = LATE + AHEAD + [(r - DATES_DEV, q - DATES_DEV) for r, q in BACK]
    for n, phase in form(load, blocks_of(pairs, [(9, 10, 11, 12), (-2, -1)])):
        stage[pl.ds(g * 256 + h * 16 + n, 8, stride=32), :] = phase
        sum_ref[n * 8:(n + 1) * 8, :] += phase

    @pl.when(step == 3)
    def _():
        total_ref[N_ALL:, :] = jnp.zeros((PAD - N_ALL, LANES), jnp.float32)
        for first, ref in ((0, early_sum_ref), (N_EARLY, sum_ref)):
            count = ref.shape[0] // 8
            total = jnp.sum(jnp.sum(ref[...].reshape(count, 8, LANES), axis=1), axis=1, keepdims=True)
            total_ref[first:first + count, :] = jnp.broadcast_to(total, (count, LANES))
        row = lax.broadcasted_iota(jnp.int32, (PAD, LANES), 0) + lax.axis_index("date") * PAD
        lane = lax.broadcasted_iota(jnp.int32, (PAD, LANES), 1)
        total = total_ref[...]
        lines = [
            jnp.sum(jnp.where(lane + i * LANES == row, total, 0.0), axis=0, keepdims=True) for i in range(8)
        ]
        for half in range(2):
            four = jnp.concatenate(lines[4 * half:4 * half + 4], axis=0)
            for l in range(LINES):
                at = (l * 2 + half) * 16 + 12
                stage[at:at + 4, :] = four
        copy = pltpu.make_async_copy(
            stage.reshape(2 * LINES, 16, LANES), out_ref.at[:, pl.ds(N_EARLY, 16), :], out_sem
        )
        copy.start()
        copy.wait()


def early_phases(slc):
    return pl.pallas_call(
        early_kernel,
        grid=(4,),
        in_specs=[pl.BlockSpec(memory_space=HBM)],
        out_specs=[
            pl.BlockSpec(memory_space=pl.ANY),
            pl.BlockSpec((8 * N_EARLY, LANES), lambda i: (0, 0)),
            pl.BlockSpec(memory_space=pltpu.VMEM),
        ],
        out_shape=[
            jax.ShapeDtypeStruct((2 * LINES, PAD, LANES), jnp.float32),
            jax.ShapeDtypeStruct((8 * N_EARLY, LANES), jnp.float32),
            jax.ShapeDtypeStruct((4, 6, 2, 128, LANES), jnp.float32),
        ],
        scratch_shapes=[
            pltpu.VMEM((4, 2, DATES_DEV, 2, 64, LANES), jnp.float32),
            pltpu.VMEM((2 * LINES * N_EARLY, LANES), jnp.float32),
            pltpu.SemaphoreType.DMA((4, 2)),
            pltpu.SemaphoreType.DMA((2,)),
            pltpu.SemaphoreType.DMA((4, 2)),
        ],
        compiler_params=pltpu.CompilerParams(vmem_limit_bytes=VMEM),
        cost_estimate=pl.CostEstimate(flops=30_000_000, bytes_accessed=8_000_000, transcendentals=0),
        name="early_pairs",
    )(slc)


def late_phases(early, early_sums, keep, up, down):
    anywhere = pl.BlockSpec(memory_space=pl.ANY)
    vmem = pl.BlockSpec(memory_space=pltpu.VMEM)
    return pl.pallas_call(
        late_kernel,
        grid=(4,),
        in_specs=[vmem, vmem, vmem, vmem, anywhere],
        out_specs=anywhere,
        out_shape=jax.ShapeDtypeStruct(early.shape, jnp.float32),
        input_output_aliases={4: 0},
        scratch_shapes=[
            pltpu.VMEM((2 * LINES * 16, LANES), jnp.float32),
            pltpu.VMEM((8 * 16, LANES), jnp.float32),
            pltpu.VMEM((PAD, LANES), jnp.float32),
            pltpu.SemaphoreType.DMA,
        ],
        compiler_params=pltpu.CompilerParams(vmem_limit_bytes=VMEM),
        cost_estimate=pl.CostEstimate(flops=10_000_000, bytes_accessed=6_000_000, transcendentals=0),
        name="late_pairs",
    )(keep, up, down, early_sums, early)


def spread_kernel(x_ref, out_ref):
    rows = [jnp.sum(x_ref[:, at + 48:at + PAD, :], axis=0)[4:] for at in (0, PAD)]
    out_ref[...] = jnp.broadcast_to(jnp.concatenate(rows, axis=0)[None], (N, 8, LANES))


def spread(x):
    return pl.pallas_call(
        spread_kernel,
        out_shape=jax.ShapeDtypeStruct((N, 8, LANES), jnp.float32),
        compiler_params=pltpu.CompilerParams(vmem_limit_bytes=VMEM),
        cost_estimate=pl.CostEstimate(flops=100_000, bytes_accessed=1_000_000, transcendentals=0),
        name="spread",
    )(x)


def product_kernel(x_ref, w_ref, out_ref, weights_ref):
    device = lax.axis_index("date")
    within = lax.broadcasted_iota(jnp.int32, (8, 256), 0)
    moved = jnp.logical_and(within >= 1, within < 4)
    parts = []
    for o in range(N):
        here = w_ref.at[(o - device) & (N - 1)]
        before = w_ref.at[(o - 1 - device) & (N - 1)]
        parts.append(here[:48, :])
        parts.append(jnp.where(moved, before[48:, :], here[48:, :]))
    weights = jnp.transpose(jnp.concatenate(parts, axis=0))[:TIMES]
    weights_ref[...] = weights
    lane = lax.broadcasted_iota(jnp.int32, (TIMES, LANES), 1)
    order = 2 * (lane % 64) + lane // 64
    for half in range(2):
        x = x_ref[:, half * PAD:(half + 1) * PAD, :].reshape(DEPTH, LANES)
        y = jnp.dot(weights, x, precision=lax.Precision.HIGHEST, preferred_element_type=jnp.float32)
        out_ref[:, half * LANES:(half + 1) * LANES] = jnp.take_along_axis(y, order, axis=1)


def product(x, w):
    return pl.pallas_call(
        product_kernel,
        out_shape=[
            jax.ShapeDtypeStruct((TIMES, 256), jnp.float32),
            jax.ShapeDtypeStruct((TIMES, DEPTH), jnp.float32),
        ],
        compiler_params=pltpu.CompilerParams(vmem_limit_bytes=VMEM),
        cost_estimate=pl.CostEstimate(flops=600_000_000, bytes_accessed=2_000_000, transcendentals=0),
        name="product",
    )(x, w)


def centre_kernel(y_ref, weights_ref, sums_ref, out_ref):
    totals = jnp.zeros((TIMES, LANES), jnp.float32)
    for i in range(DEPTH // LANES):
        line = jnp.sum(sums_ref[:, i, :], axis=0, keepdims=True)
        totals += weights_ref[:, i * LANES:(i + 1) * LANES] * line
    offset = jnp.sum(totals, axis=1, keepdims=True) * (1.0 / (LINES * 4096))
    out_ref[:, 0, :] = (y_ref[...] - offset)[:207]


def centre(y, weights, sums):
    return pl.pallas_call(
        centre_kernel,
        out_shape=jax.ShapeDtypeStruct((207, 1, 256), jnp.float32),
        compiler_params=pltpu.CompilerParams(vmem_limit_bytes=VMEM),
        cost_estimate=pl.CostEstimate(flops=400_000, bytes_accessed=1_200_000, transcendentals=0),
        name="centre",
    )(y, weights, sums)


def per_device(slc, pair_slots, inversion):
    slc = pltpu.with_memory_space_constraint(slc, HBM)
    head, tail = edges(slc)
    up = lax.ppermute(head, "date", [(i + 1, i) for i in range(N - 1)])
    down = lax.ppermute(tail, "date", [(i, i + 1) for i in range(N - 1)])
    early, early_sums, keep = early_phases(slc)
    pair_slots, inversion, early_sums = lax.optimization_barrier((pair_slots, inversion, early_sums))
    w = ordered_weights(pair_slots, inversion)
    w = lax.ppermute(w, ("date", "tile"), [(o * N + j, (o - j) % N * N + j) for o in range(N) for j in range(N)])

    payload = late_phases(early, early_sums, keep, up, down)
    w, payload = lax.optimization_barrier((w, payload))
    x = lax.all_to_all(payload.reshape(LINES, ROWS, LANES), "date", 0, 0, tiled=True)
    w = lax.all_gather(w, "tile", axis=0)
    rows, w = lax.optimization_barrier((spread(x), w))
    sums = lax.all_to_all(rows, "tile", 0, 0, tiled=True)
    return jnp.swapaxes(centre(*product(x, w), sums), 0, 1)


def solution(mesh):
    return jax.shard_map(
        per_device,
        mesh=mesh,
        in_specs=(P("date", None, None, "tile"), P("date", None), P(None, "date")),
        out_specs=P("date", None, "tile"),
        check_vma=False,
    )
```
